32 devices in a mesh: groups: 2 (over y), dp: 4 (over z), tensor: 2 (over x), seq: 2 (over core).
Axes of the slice: x: 2, y: 2, z: 4, core: 2. Of those that a mesh axis runs over, the one named last changes fastest.
Arguments:
- activations: bfloat16 [8, 512, 4096], P(('groups', 'dp'), 'seq', 'tensor'), parts along dimension 0, may hold values from -6 to 6
- gate_input: bfloat16 [8, 512, 7168], P(('groups', 'dp'), None, ('tensor', 'seq')), parts along dimension 0, may hold values from -8 to 8
- out_grad: bfloat16 [8, 512, 4096], P(('groups', 'dp'), 'seq'), parts along dimension 0, may hold values from -6 to 6
- down_weight: bfloat16 [7168, 4096], P(('tensor', 'seq')), may hold values from -0.0625 to 0.0625
- proj_in: bfloat16 [4096, 64], P('tensor'), may hold values from -0.09375 to 0.09375
- proj_out: bfloat16 [7168, 64], P(('tensor', 'seq')), may hold values from -0.125 to 0.125
- precond_in: float32 [64, 64], replicated, may hold values from -1 to 2, as said below
- precond_out: float32 [64, 64], replicated, may hold values from -1 to 2, as said below
- queries: float32 [128, 4096], P(('groups', 'dp')), parts along dimension 0, may hold values from -6 to 6
Outputs:
- scores: float32 [8, 64], P(('groups', 'dp')), parts along dimension 0
The draws below stay inside these ranges and needn't reach their ends.
There are 2 independent parts, one for each index of `groups`. The reference program is written for one: setup_inputs(seed, part) draws one part's arguments, and reference() takes and returns one part's arrays. A program takes and returns all parts, laid end to end along the dimension named above; an argument that names none is the same for every part. Nothing has to cross between parts.
Inputs may be any that keep to these rules, and one draw needn't show every extreme that they name: `precond_in`: symmetric. `precond_out`: symmetric.
All inputs are finite; a program needn't handle non-finite values.
Results may differ from the reference program's by a relative error of at most 0.0028.
Values may be sent and summed in bfloat16 or wider, within the bound.
A program may use at most 64 MiB of HBM per device.

```python
import math
import jax
import jax.numpy as jnp
from jax import lax

D = 4096
FF = 7168
K1 = 64
K2 = 64
LEN = 512
EX = 4
NQ = 64


def symmetric_factor(key, order):
    noise = jnp.clip(jax.random.normal(key, (order, order), jnp.float32), -4.0, 4.0)
    noise = noise * (0.3 / jnp.sqrt(jnp.float32(order)))
    return jnp.eye(order, dtype=jnp.float32) + noise + noise.T


def draw_precond_in(key, part):
    key = jax.random.fold_in(key, 11)
    return symmetric_factor(key, K1)


def draw_precond_out(key, part):
    key = jax.random.fold_in(key, 23)
    return symmetric_factor(key, K2)


def levels(key, dims, pieces, smallest, top_value):
    level = 1.0
    for position, parts in pieces:
        draws = jax.random.uniform(jax.random.fold_in(jax.random.fold_in(key, 6), position), (parts,), jnp.float32, smallest / len(pieces), top_value / len(pieces))
        level = level * jnp.repeat(jnp.exp(draws), dims[position] // parts).reshape((-1,) + (1,) * (len(dims) - 1 - position))
    return level


def gaussian(stream_key, dims, width, bound, shards=(), held_as=jnp.bfloat16):
    array = jax.random.normal(stream_key, dims, jnp.float32) * width
    if len(shards) > 0:
        array = levels(stream_key, dims, shards, -0.22, 0.18) * array
    return jnp.clip(array, min=-bound, max=bound).astype(held_as)


def setup_inputs(seed: int = 0, part: int = 0) -> dict:
    splits = jax.random.split(jax.random.key(seed), 10)
    own_keys = jax.random.split(jax.random.fold_in(splits[9], part), 10)
    return {
        "activations": gaussian(own_keys[0], (EX, LEN, D), 1.0, 6.0, ((0, 4), (1, 2), (2, 2))),
        "gate_input": gaussian(own_keys[1], (EX, LEN, FF), 1.5, 8.0, ((0, 4), (2, 4))),
        "out_grad": gaussian(own_keys[2], (EX, LEN, D), 1.0, 6.0, ((0, 4), (1, 2))),
        "down_weight": gaussian(splits[3], (FF, D), FF ** -0.5, 0.0625, ((0, 4),)),
        "proj_in": gaussian(splits[4], (D, K1), D ** -0.5, 0.09375, ((0, 2),)),
        "proj_out": gaussian(splits[5], (FF, K2), (FF // 4) ** -0.5, 0.125, ((0, 4),)),
        "precond_in": draw_precond_in(jax.random.fold_in(splits[9], 71), part),
        "precond_out": draw_precond_out(jax.random.fold_in(splits[9], 71), part),
        "queries": gaussian(own_keys[8], (NQ, K1 * K2), 1.0, 6.0, ((0, 4),), jnp.float32),
    }


def reference(activations, gate_input, out_grad, down_weight, proj_in, proj_out, precond_in, precond_out, queries):
    down_full = down_weight.astype(jnp.float32)
    proj_in_full = proj_in.astype(jnp.float32)
    proj_out_full = proj_out.astype(jnp.float32)

    def per_example(items):
        act_rows, gate_rows, grad_rows = items
        hid_grad = jnp.dot(grad_rows.astype(jnp.float32), down_full.T, precision=lax.Precision.HIGHEST)
        up_grad = (hid_grad * jax.nn.silu(gate_rows.astype(jnp.float32))).astype(jnp.bfloat16)
        left_factor = jnp.dot(act_rows.astype(jnp.float32), proj_in_full, precision=lax.Precision.HIGHEST)
        right_factor = jnp.dot(up_grad.astype(jnp.float32), proj_out_full, precision=lax.Precision.HIGHEST)
        example_grad = jnp.dot(left_factor.T, right_factor, precision=lax.Precision.HIGHEST)
        section_one = jnp.dot(precond_in, example_grad, precision=lax.Precision.HIGHEST)
        precond_grad = jnp.dot(section_one, precond_out, precision=lax.Precision.HIGHEST)
        return precond_grad.reshape(-1)
    flattened = lax.map(per_example, (activations, gate_input, out_grad))
    score_scale = 1.0 / math.sqrt(LEN * K1 * K2)
    return jnp.dot(flattened, queries.T, precision=lax.Precision.HIGHEST) * score_scale
```

```python
import functools
import math

import jax
import jax.numpy as jnp
from jax import lax
from jax.experimental import pallas as pl
from jax.experimental.pallas import tpu as pltpu
from jax.sharding import PartitionSpec as P

MESH = pl.DeviceIdType.MESH
F32 = jnp.float32
BF16 = jnp.bfloat16
NT = (((1,), (1,)), ((), ()))
NN = (((1,), (0,)), ((), ()))


def split(x):
    hi = x.astype(BF16)
    return hi, (x - hi.astype(F32)).astype(BF16)


def kernel(
    dims, scale,
    act_h, gate_h, grad_h, down_h, pin_h, pout_h, cin_h, cout_h, query_h,
    out_ref,
    down, grad, gate, act, pin, pout, pout2, cin, cout, query, qsend, qall,
    lefts, rights, scores,
    down_sem, load_sem,
    grad_sem, left_send, left_recv, q_send, q_recv, qc_send, qc_recv, s_send, s_recv,
):
    groups, dp, tensor, seq, chunk = dims
    ff = down.shape[0]
    chunks = ff // chunk
    tokens = grad.shape[1]
    k1 = cin.shape[0]
    half = qsend.shape[1]
    nq_block = qsend.shape[0]
    ranks = tensor * seq
    g, z = lax.axis_index("groups"), lax.axis_index("dp")
    x, s = lax.axis_index("tensor"), lax.axis_index("seq")
    me = x * seq + s
    other = 1 - s

    def peer(k):
        r = lax.rem(me + k, ranks)
        return (g, z, r // seq, lax.rem(r, seq))

    def along(k):
        return (g, lax.rem(z + k, dp), x, s)

    barrier = pltpu.get_barrier_semaphore()
    for k in range(1, ranks):
        pl.semaphore_signal(barrier, inc=1, device_id=peer(k), device_id_type=MESH)
    for k in range(1, dp):
        pl.semaphore_signal(barrier, inc=1, device_id=along(k), device_id_type=MESH)

    def rows_of(c):
        return pl.ds(pl.multiple_of(c * chunk, chunk), chunk)

    def load(src, dst, i):
        copy = pltpu.make_async_copy(src, dst, load_sem.at[i])
        copy.start()
        return copy

    def down_copy(c):
        return pltpu.make_async_copy(
            down_h.at[rows_of(c)], down.at[rows_of(c)], down_sem.at[c]
        )

    def token_rows(b):
        return pl.ds(pl.multiple_of(b * tokens, tokens), tokens)

    get_query = load(query_h, query, 0)
    get_act = load(act_h.at[0], act, 1)
    get_pin = load(pin_h, pin, 2)
    get_cin = load(cin_h, cin, 3)
    get_cout = load(cout_h, cout, 4)
    get_pout = load(pout_h, pout, 5)
    get_grad = load(grad_h.at[0], grad.at[0], 6)
    get_gate0 = load(gate_h.at[0, token_rows(s)], gate.at[0], 7)
    for c in range(chunks):
        down_copy(c).start()
    get_gate1 = load(gate_h.at[0, token_rows(other)], gate.at[1], 8)

    pl.semaphore_wait(barrier, ranks - 1 + dp - 1)

    send_grad = pltpu.make_async_remote_copy(
        src_ref=grad_h.at[0], dst_ref=grad.at[1],
        send_sem=grad_sem.at[0], recv_sem=grad_sem.at[1],
        device_id=(g, z, x, other), device_id_type=MESH,
    )
    send_grad.start()

    get_query.wait()
    for h in range(seq):
        qall[z, h] = query[:, h * half:(h + 1) * half].astype(BF16)

    def q_copy(k, block):
        return pltpu.make_async_remote_copy(
            src_ref=qall.at[z, s], dst_ref=qall.at[block, s],
            send_sem=q_send.at[k], recv_sem=q_recv.at[block],
            device_id=along(k), device_id_type=MESH,
        )

    for k in range(1, dp):
        q_copy(k, z).start()

    get_act.wait()
    get_pin.wait()
    get_cin.wait()
    left = lax.dot_general(act[...], pin[...], NN, preferred_element_type=F32)
    cin_rows = jnp.concatenate(
        [cin[pl.ds(0, k1 // 2, 2), :], cin[pl.ds(1, k1 // 2, 2), :]], axis=0
    )
    lefts[me] = lax.dot_general(
        cin_rows, left, NT, precision=lax.Precision.HIGHEST, preferred_element_type=F32
    )

    def left_copy(k, rank):
        return pltpu.make_async_remote_copy(
            src_ref=lefts.at[me], dst_ref=lefts.at[rank],
            send_sem=left_send.at[k], recv_sem=left_recv.at[rank],
            device_id=peer(k), device_id_type=MESH,
        )

    for k in range(1, ranks):
        left_copy(k, me).start()

    get_cout.wait()
    get_pout.wait()
    cout2 = jnp.concatenate(split(cout[...]), axis=1)
    k2 = cout.shape[0]

    def project(c):
        y = lax.dot_general(pout[rows_of(c), :], cout2, NN, preferred_element_type=F32)
        pout2[rows_of(c), :] = jnp.concatenate(split(y[:, :k2] + y[:, k2:]), axis=1)

    def step(phase, c):
        hid = lax.dot_general(
            grad[phase], down[rows_of(c), :], NT, preferred_element_type=F32
        )
        v = gate[phase, :, rows_of(c)].astype(F32)
        up = (hid * (v / (1.0 + jnp.exp(-v)))).astype(BF16)
        rights[phase] += lax.dot_general(
            up, pout2[rows_of(c), :], NN, preferred_element_type=F32
        )

    rights[...] = jnp.zeros_like(rights)
    get_grad.wait()
    get_gate0.wait()

    @pl.loop(0, chunks)
    def _(c):
        project(c)
        down_copy(c).wait()
        step(0, c)

    get_gate1.wait()
    send_grad.wait()

    def qc_copy(block, owner):
        return pltpu.make_async_remote_copy(
            src_ref=qall.at[block, owner], dst_ref=qall.at[block, owner],
            send_sem=qc_send.at[block], recv_sem=qc_recv.at[block],
            device_id=(g, z, x, other), device_id_type=MESH,
        )

    for k in range(1, dp):
        block = lax.rem(z + dp - k, dp)
        q_copy(k, block).wait_recv()
        qc_copy(block, s).start()

    for k in range(1, ranks):
        left_copy(k, lax.rem(me + ranks - k, ranks)).wait_recv()

    @pl.loop(0, chunks)
    def _(c):
        step(1, c)

    def product(phase, block):
        total = lefts[block]
        for t in range(1, tensor):
            total = total + lefts[t * seq + block]
        l2 = jnp.concatenate(split(total), axis=0)
        r2 = jnp.concatenate(split(rights[phase]), axis=1)
        return lax.dot_general(l2, r2, NN, preferred_element_type=F32)

    m = product(0, s) + product(1, other)
    m = m[:k1] + m[k1:]
    m = m[:, :2 * k2] + m[:, 2 * k2:]
    m = (m[:, :k2] + m[:, k2:]) * scale
    wide = jnp.concatenate([m[:k1 // 2], m[k1 // 2:]], axis=1)

    for k in range(1, dp):
        block = lax.rem(z + dp - k, dp)
        qc_copy(block, other).wait_recv()

    lanes = 2 * k2
    rows = half // lanes
    sums = []
    for b in range(dp):
        acc = jnp.zeros((nq_block, lanes), F32)
        for h in range(seq):
            for r in range(rows):
                i = h * rows + r
                acc = acc + wide[i:i + 1, :] * qall[b, h, :, r * lanes:(r + 1) * lanes].astype(F32)
        sums.append(acc)
    acc = jnp.concatenate(sums, axis=0)
    row = jnp.sum(acc.T, axis=0, keepdims=True)
    scores[me] = jnp.broadcast_to(row, scores.shape[1:])

    def score_copy(k, rank):
        return pltpu.make_async_remote_copy(
            src_ref=scores.at[me], dst_ref=scores.at[rank],
            send_sem=s_send.at[k], recv_sem=s_recv.at[rank],
            device_id=peer(k), device_id_type=MESH,
        )

    for k in range(1, ranks):
        score_copy(k, me).start()
    for k in range(1, ranks):
        score_copy(k, lax.rem(me + ranks - k, ranks)).wait_recv()
    total = scores[0, 0:1]
    for r in range(1, ranks):
        total = total + scores[r, 0:1]
    out_ref[...] = total

    for k in range(1, ranks):
        score_copy(k, me).wait_send()
        left_copy(k, me).wait_send()
    for k in range(1, dp):
        q_copy(k, z).wait_send()
        qc_copy(lax.rem(z + dp - k, dp), s).wait_send()


def solution(mesh):
    shape = dict(mesh.shape)
    groups, dp, tensor, seq = (shape[a] for a in ("groups", "dp", "tensor", "seq"))

    def body(act, gate, grad, down, pin, pout, cin, cout, query):
        tokens, d_local = act.shape[1:]
        features = grad.shape[2]
        ff = down.shape[0]
        k1, k2 = pin.shape[1], pout.shape[1]
        nq_block, width = query.shape
        chunk = next(c for c in (256, 128) if ff % c == 0 and ff // c >= 4)
        chunks = ff // chunk
        ranks = tensor * seq
        nq = nq_block * dp
        scale = 1.0 / math.sqrt(gate.shape[1] * k1 * k2)
        dma = pltpu.SemaphoreType.DMA
        scratch = [
            pltpu.VMEM((ff, features), BF16),
            pltpu.VMEM((2, tokens, features), BF16),
            pltpu.VMEM((2, tokens, ff), BF16),
            pltpu.VMEM((tokens, d_local), BF16),
            pltpu.VMEM((d_local, k1), BF16),
            pltpu.VMEM((ff, k2), BF16),
            pltpu.VMEM((ff, 2 * k2), BF16),
            pltpu.VMEM((k1, k1), F32),
            pltpu.VMEM((k2, k2), F32),
            pltpu.VMEM((nq_block, width), F32),
            pltpu.VMEM((nq_block, width // seq), BF16),
            pltpu.VMEM((dp, seq, nq_block, width // seq), BF16),
            pltpu.VMEM((ranks, k1, tokens), F32),
            pltpu.VMEM((2, tokens, 2 * k2), F32),
            pltpu.VMEM((ranks, 8, nq), F32),
            dma((chunks,)),
            dma((9,)),
            dma((2,)),
            dma((ranks,)), dma((ranks,)),
            dma((dp,)), dma((dp,)),
            dma((dp,)), dma((dp,)),
            dma((ranks,)), dma((ranks,)),
        ]
        return pl.pallas_call(
            functools.partial(kernel, (groups, dp, tensor, seq, chunk), scale),
            out_shape=jax.ShapeDtypeStruct((1, nq), F32),
            in_specs=[pl.BlockSpec(memory_space=pl.ANY)] * 9,
            out_specs=pl.BlockSpec(memory_space=pltpu.VMEM),
            scratch_shapes=scratch,
            compiler_params=pltpu.CompilerParams(
                collective_id=0, has_side_effects=True, vmem_limit_bytes=58 * 2**20
            ),
            cost_estimate=pl.CostEstimate(
                flops=4 * tokens * ff * features,
                bytes_accessed=2 * ff * features,
                transcendentals=0,
            ),
        )(act, gate, grad, down, pin, pout, cin, cout, query)

    return jax.shard_map(
        body,
        mesh=mesh,
        in_specs=(
            P(("groups", "dp"), "seq", "tensor"),
            P(("groups", "dp"), None, ("tensor", "seq")),
            P(("groups", "dp"), "seq", None),
            P(("tensor", "seq"), None),
            P("tensor", None),
            P(("tensor", "seq"), None),
            P(),
            P(),
            P(("groups", "dp"), None),
        ),
        out_specs=P(("groups", "dp"), None),
        check_vma=False,
    )
```

```python
import functools
import math

import jax
import jax.numpy as jnp
from jax import lax
from jax.experimental import pallas as pl
from jax.experimental.pallas import tpu as pltpu
from jax.sharding import PartitionSpec as P

MESH = pl.DeviceIdType.MESH
F32 = jnp.float32
BF16 = jnp.bfloat16
NT = (((1,), (1,)), ((), ()))
NN = (((1,), (0,)), ((), ()))


def split(x):
    hi = x.astype(BF16)
    return hi, (x - hi.astype(F32)).astype(BF16)


def kernel(
    dims, scale,
    act_h, gate_h, grad_h, down_h, pin_h, pout_h, cin_h, cout_h, query_h,
    out_ref,
    down, grad, gate, act, pin, pout, cin, cout, query, qall,
    lefts, scores,
    down_sem, load_sem,
    grad_sem, left_send, left_recv, q_send, q_recv, qc_send, qc_recv, s_send, s_recv,
):
    groups, dp, tensor, seq, chunk = dims
    ff = down.shape[0]
    chunks = ff // chunk
    tokens = grad.shape[1]
    k1 = cin.shape[0]
    nq_block = query.shape[0]
    half = query.shape[1] // seq
    ranks = tensor * seq
    g, z = lax.axis_index("groups"), lax.axis_index("dp")
    x, s = lax.axis_index("tensor"), lax.axis_index("seq")
    me = x * seq + s
    other = 1 - s

    def peer(k):
        r = lax.rem(me + k, ranks)
        return (g, z, r // seq, lax.rem(r, seq))

    def along(k):
        return (g, lax.rem(z + k, dp), x, s)

    barrier = pltpu.get_barrier_semaphore()
    for k in range(1, ranks):
        pl.semaphore_signal(barrier, inc=1, device_id=peer(k), device_id_type=MESH)
    for k in range(1, dp):
        pl.semaphore_signal(barrier, inc=1, device_id=along(k), device_id_type=MESH)

    def rows_of(c):
        return pl.ds(pl.multiple_of(c * chunk, chunk), chunk)

    def load(src, dst, i):
        copy = pltpu.make_async_copy(src, dst, load_sem.at[i])
        copy.start()
        return copy

    def down_copy(c):
        return pltpu.make_async_copy(
            down_h.at[rows_of(c)], down.at[rows_of(c)], down_sem.at[c]
        )

    def token_rows(b):
        return pl.ds(pl.multiple_of(b * tokens, tokens), tokens)

    get_act = load(act_h.at[0], act, 1)
    get_pin = load(pin_h, pin, 2)
    get_query = load(query_h, query, 0)
    get_cin = load(cin_h, cin, 3)
    get_cout = load(cout_h, cout, 4)
    get_pout = load(pout_h, pout, 5)
    get_grad = load(grad_h.at[0], grad.at[0], 6)
    down_copy(0).start()
    get_gate0 = load(gate_h.at[0, token_rows(s)], gate.at[0], 7)
    for c in range(1, chunks):
        down_copy(c).start()
    get_gate1 = load(gate_h.at[0, token_rows(other)], gate.at[1], 8)

    pl.semaphore_wait(barrier, ranks - 1 + dp - 1)

    send_grad = pltpu.make_async_remote_copy(
        src_ref=grad_h.at[0], dst_ref=grad.at[1],
        send_sem=grad_sem.at[0], recv_sem=grad_sem.at[1],
        device_id=(g, z, x, other), device_id_type=MESH,
    )
    send_grad.start()

    get_query.wait()
    for h in range(seq):
        qall[z, h] = query[:, h * half:(h + 1) * half].astype(BF16)

    def q_copy(k, block):
        return pltpu.make_async_remote_copy(
            src_ref=qall.at[z, s], dst_ref=qall.at[block, s],
            send_sem=q_send.at[k], recv_sem=q_recv.at[block],
            device_id=along(k), device_id_type=MESH,
        )

    for k in range(1, dp):
        q_copy(k, z).start()

    get_act.wait()
    get_pin.wait()
    get_cin.wait()
    left = lax.dot_general(pin[...], act[...], NT, preferred_element_type=F32)
    cin_rows = jnp.concatenate(
        [cin[pl.ds(0, k1 // 2, 2), :], cin[pl.ds(1, k1 // 2, 2), :]], axis=0
    )
    lefts[me] = lax.dot_general(
        cin_rows, left, NN, precision=lax.Precision.HIGHEST, preferred_element_type=F32
    )

    def left_copy(k, rank):
        return pltpu.make_async_remote_copy(
            src_ref=lefts.at[me], dst_ref=lefts.at[rank],
            send_sem=left_send.at[k], recv_sem=left_recv.at[rank],
            device_id=peer(k), device_id_type=MESH,
        )

    for k in range(1, ranks):
        left_copy(k, me).start()

    get_cout.wait()
    get_pout.wait()
    k2 = cout.shape[0]
    cout2 = jnp.concatenate(split(cout[...]), axis=0)
    y = lax.dot_general(cout2, pout[...], NN, preferred_element_type=F32)
    pout2 = jnp.concatenate(split(y[:k2] + y[k2:]), axis=0)

    def step(phase, c):
        rows = slice(c * chunk, (c + 1) * chunk)
        hid = lax.dot_general(down[rows, :], grad[phase], NT, preferred_element_type=F32)
        v = gate[phase, :, rows].astype(F32).T
        up = (hid * (v / (1.0 + jnp.exp(-v)))).astype(BF16)
        return lax.dot_general(pout2[:, rows], up, NN, preferred_element_type=F32)

    get_grad.wait()
    get_gate0.wait()
    right0 = 0.0
    for c in range(chunks):
        down_copy(c).wait()
        right0 = right0 + step(0, c)

    get_gate1.wait()
    send_grad.wait()

    def qc_copy(block, owner):
        return pltpu.make_async_remote_copy(
            src_ref=qall.at[block, owner], dst_ref=qall.at[block, owner],
            send_sem=qc_send.at[block], recv_sem=qc_recv.at[block],
            device_id=(g, z, x, other), device_id_type=MESH,
        )

    for k in range(1, dp):
        block = lax.rem(z + dp - k, dp)
        q_copy(k, block).wait_recv()
        qc_copy(block, s).start()

    for k in range(1, ranks):
        left_copy(k, lax.rem(me + ranks - k, ranks)).wait_recv()

    def product(right, block):
        total = lefts[block]
        for r in range(1, tensor):
            total = total + lefts[r * seq + block]
        l2 = jnp.concatenate(split(total), axis=0)
        r2 = jnp.concatenate(split(right), axis=0)
        return lax.dot_general(l2, r2, NT, preferred_element_type=F32)

    m = product(right0, s)
    right1 = 0.0
    for c in range(chunks):
        right1 = right1 + step(1, c)
    m = m + product(right1, other)
    m = m[:k1] + m[k1:]
    m = m[:, :2 * k2] + m[:, 2 * k2:]
    m = (m[:, :k2] + m[:, k2:]) * scale
    wide = jnp.concatenate([m[:k1 // 2], m[k1 // 2:]], axis=1)

    for k in range(1, dp):
        block = lax.rem(z + dp - k, dp)
        qc_copy(block, other).wait_recv()

    lanes = 2 * k2
    rows = half // lanes
    sums = []
    for b in range(dp):
        acc = jnp.zeros((nq_block, lanes), F32)
        for h in range(seq):
            for r in range(rows):
                i = h * rows + r
                acc = acc + wide[i:i + 1, :] * qall[b, h, :, r * lanes:(r + 1) * lanes].astype(F32)
        sums.append(acc)
    acc = jnp.concatenate(sums, axis=0)
    row = jnp.sum(acc.T, axis=0, keepdims=True)
    scores[me] = jnp.broadcast_to(row, scores.shape[1:])

    def score_copy(k, rank):
        return pltpu.make_async_remote_copy(
            src_ref=scores.at[me], dst_ref=scores.at[rank],
            send_sem=s_send.at[k], recv_sem=s_recv.at[rank],
            device_id=peer(k), device_id_type=MESH,
        )

    for k in range(1, ranks):
        score_copy(k, me).start()
    for k in range(1, ranks):
        score_copy(k, lax.rem(me + ranks - k, ranks)).wait_recv()
    total = scores[0, 0:1]
    for r in range(1, ranks):
        total = total + scores[r, 0:1]
    out_ref[...] = total

    for k in range(1, ranks):
        score_copy(k, me).wait_send()
        left_copy(k, me).wait_send()
    for k in range(1, dp):
        q_copy(k, z).wait_send()
        qc_copy(lax.rem(z + dp - k, dp), s).wait_send()


def solution(mesh):
    shape = dict(mesh.shape)
    groups, dp, tensor, seq = (shape[a] for a in ("groups", "dp", "tensor", "seq"))

    def body(act, gate, grad, down, pin, pout, cin, cout, query):
        tokens, d_local = act.shape[1:]
        features = grad.shape[2]
        ff = down.shape[0]
        pin, pout = pin.T, pout.T
        k1, k2 = pin.shape[0], pout.shape[0]
        nq_block, width = query.shape
        chunk = next(c for c in (896, 512, 256, 128) if ff % c == 0)
        chunks = ff // chunk
        ranks = tensor * seq
        nq = nq_block * dp
        scale = 1.0 / math.sqrt(gate.shape[1] * k1 * k2)
        dma = pltpu.SemaphoreType.DMA
        scratch = [
            pltpu.VMEM((ff, features), BF16),
            pltpu.VMEM((2, tokens, features), BF16),
            pltpu.VMEM((2, tokens, ff), BF16),
            pltpu.VMEM((tokens, d_local), BF16),
            pltpu.VMEM((k1, d_local), BF16),
            pltpu.VMEM((k2, ff), BF16),
            pltpu.VMEM((k1, k1), F32),
            pltpu.VMEM((k2, k2), F32),
            pltpu.VMEM((nq_block, width), F32),
            pltpu.VMEM((dp, seq, nq_block, width // seq), BF16),
            pltpu.VMEM((ranks, k1, tokens), F32),
            pltpu.VMEM((ranks, 8, nq), F32),
            dma((chunks,)),
            dma((9,)),
            dma((2,)),
            dma((ranks,)), dma((ranks,)),
            dma((dp,)), dma((dp,)),
            dma((dp,)), dma((dp,)),
            dma((ranks,)), dma((ranks,)),
        ]
        return pl.pallas_call(
            functools.partial(kernel, (groups, dp, tensor, seq, chunk), scale),
            out_shape=jax.ShapeDtypeStruct((1, nq), F32),
            in_specs=[pl.BlockSpec(memory_space=pl.ANY)] * 9,
            out_specs=pl.BlockSpec(memory_space=pltpu.VMEM),
            scratch_shapes=scratch,
            compiler_params=pltpu.CompilerParams(
                collective_id=0, has_side_effects=True, vmem_limit_bytes=58 * 2**20
            ),
            cost_estimate=pl.CostEstimate(
                flops=4 * tokens * ff * features,
                bytes_accessed=2 * ff * features,
                transcendentals=0,
            ),
        )(act, gate, grad, down, pin, pout, cin, cout, query)

    return jax.shard_map(
        body,
        mesh=mesh,
        in_specs=(
            P(("groups", "dp"), "seq", "tensor"),
            P(("groups", "dp"), None, ("tensor", "seq")),
            P(("groups", "dp"), "seq", None),
            P(("tensor", "seq"), None),
            P("tensor", None),
            P(("tensor", "seq"), None),
            P(),
            P(),
            P(("groups", "dp"), None),
        ),
        out_specs=P(("groups", "dp"), None),
        check_vma=False,
    )
```

```python
import functools
import math

import jax
import jax.numpy as jnp
from jax import lax
from jax.experimental import pallas as pl
from jax.experimental.pallas import tpu as pltpu
from jax.sharding import PartitionSpec as P

MESH = pl.DeviceIdType.MESH
F32 = jnp.float32
BF16 = jnp.bfloat16
NT = (((1,), (1,)), ((), ()))
NN = (((1,), (0,)), ((), ()))


def split(x):
    hi = x.astype(BF16)
    return hi, (x - hi.astype(F32)).astype(BF16)


def kernel(
    dims, scale,
    act_h, gate_h, grad_h, down_h, pin_h, pout_h, cin_h, cout_h, query_h,
    out_ref,
    down, grad, gate, act, pin, pout, cin, cout, query, qall,
    lefts, scores,
    down_sem, load_sem,
    grad_sem, left_send, left_recv, q_send, q_recv, qc_send, qc_recv, s_send, s_recv,
):
    groups, dp, tensor, seq, first, second = dims
    tokens = grad.shape[1]
    k1 = cin.shape[0]
    nq_block = query.shape[0]
    half = query.shape[1] // seq
    ranks = tensor * seq
    g, z = lax.axis_index("groups"), lax.axis_index("dp")
    x, s = lax.axis_index("tensor"), lax.axis_index("seq")
    me = x * seq + s
    other = 1 - s

    def peer(k):
        r = lax.rem(me + k, ranks)
        return (g, z, r // seq, lax.rem(r, seq))

    def along(k):
        return (g, lax.rem(z + k, dp), x, s)

    barrier = pltpu.get_barrier_semaphore()
    for k in range(1, ranks):
        pl.semaphore_signal(barrier, inc=1, device_id=peer(k), device_id_type=MESH)
    for k in range(1, dp):
        pl.semaphore_signal(barrier, inc=1, device_id=along(k), device_id_type=MESH)

    def load(src, dst, i):
        copy = pltpu.make_async_copy(src, dst, load_sem.at[i])
        copy.start()
        return copy

    def down_copy(c):
        rows = pl.ds(*first[c])
        return pltpu.make_async_copy(down_h.at[rows], down.at[rows], down_sem.at[c])

    def token_rows(b):
        return pl.ds(pl.multiple_of(b * tokens, tokens), tokens)

    get_query = load(query_h, query, 0)
    get_act = load(act_h.at[0], act, 1)
    get_pin = load(pin_h, pin, 2)
    get_cin = load(cin_h, cin, 3)
    get_cout = load(cout_h, cout, 4)
    get_pout = load(pout_h, pout, 5)
    get_grad = load(grad_h.at[0], grad.at[0], 6)
    down_copy(0).start()
    get_gate0 = load(gate_h.at[0, token_rows(s)], gate.at[0], 7)
    for c in range(1, len(first)):
        down_copy(c).start()
    get_gate1 = load(gate_h.at[0, token_rows(other)], gate.at[1], 8)

    pl.semaphore_wait(barrier, ranks - 1 + dp - 1)

    send_grad = pltpu.make_async_remote_copy(
        src_ref=grad_h.at[0], dst_ref=grad.at[1],
        send_sem=grad_sem.at[0], recv_sem=grad_sem.at[1],
        device_id=(g, z, x, other), device_id_type=MESH,
    )
    send_grad.start()

    get_query.wait()
    for h in range(seq):
        qall[z, h] = query[:, h * half:(h + 1) * half].astype(BF16)

    def q_copy(k, block):
        return pltpu.make_async_remote_copy(
            src_ref=qall.at[z, s], dst_ref=qall.at[block, s],
            send_sem=q_send.at[k], recv_sem=q_recv.at[block],
            device_id=along(k), device_id_type=MESH,
        )

    for k in range(1, dp):
        q_copy(k, z).start()

    get_act.wait()
    get_pin.wait()
    get_cin.wait()
    left = lax.dot_general(pin[...], act[...], NT, preferred_element_type=F32)
    cin_rows = jnp.concatenate(
        [cin[pl.ds(0, k1 // 2, 2), :], cin[pl.ds(1, k1 // 2, 2), :]], axis=0
    )
    lefts[me] = lax.dot_general(
        cin_rows, left, NN, precision=lax.Precision.HIGHEST, preferred_element_type=F32
    )

    def left_copy(k, rank):
        return pltpu.make_async_remote_copy(
            src_ref=lefts.at[me], dst_ref=lefts.at[rank],
            send_sem=left_send.at[k], recv_sem=left_recv.at[rank],
            device_id=peer(k), device_id_type=MESH,
        )

    get_cout.wait()
    get_pout.wait()
    k2 = cout.shape[0]
    cout2 = jnp.concatenate(split(cout[...]), axis=0)
    y = lax.dot_general(cout2, pout[...], NN, preferred_element_type=F32)
    pout2 = jnp.concatenate(split(y[:k2] + y[k2:]), axis=0)

    for k in range(1, ranks):
        left_copy(k, me).start()

    def step(phase, start, size):
        rows = slice(start, start + size)
        hid = lax.dot_general(down[rows, :], grad[phase], NT, preferred_element_type=F32)
        v = gate[phase, :, rows].astype(F32).T
        up = (hid * (v / (1.0 + jnp.exp(-v)))).astype(BF16)
        return lax.dot_general(pout2[:, rows], up, NN, preferred_element_type=F32)

    get_grad.wait()
    get_gate0.wait()
    right0 = 0.0
    for c in range(len(first)):
        down_copy(c).wait()
        right0 = right0 + step(0, *first[c])

    get_gate1.wait()
    send_grad.wait()

    def qc_copy(block, owner):
        return pltpu.make_async_remote_copy(
            src_ref=qall.at[block, owner], dst_ref=qall.at[block, owner],
            send_sem=qc_send.at[block], recv_sem=qc_recv.at[block],
            device_id=(g, z, x, other), device_id_type=MESH,
        )

    for k in range(1, dp):
        block = lax.rem(z + dp - k, dp)
        q_copy(k, block).wait_recv()
        qc_copy(block, s).start()

    for k in range(1, ranks):
        left_copy(k, lax.rem(me + ranks - k, ranks)).wait_recv()

    def product(right, block):
        total = lefts[block]
        for r in range(1, tensor):
            total = total + lefts[r * seq + block]
        l2 = jnp.concatenate(split(total), axis=0)
        r2 = jnp.concatenate(split(right), axis=0)
        return lax.dot_general(l2, r2, NT, preferred_element_type=F32)

    m = product(right0, s)
    right1 = 0.0
    for piece in second:
        right1 = right1 + step(1, *piece)
    m = m + product(right1, other)
    m = m[:k1] + m[k1:]
    m = m[:, :2 * k2] + m[:, 2 * k2:]
    m = (m[:, :k2] + m[:, k2:]) * scale
    wide = jnp.concatenate([m[:k1 // 2], m[k1 // 2:]], axis=1)

    for k in range(1, dp):
        block = lax.rem(z + dp - k, dp)
        qc_copy(block, other).wait_recv()

    lanes = 2 * k2
    rows = half // lanes
    sums = []
    for b in range(dp):
        acc = jnp.zeros((nq_block, lanes), F32)
        for h in range(seq):
            for r in range(rows):
                i = h * rows + r
                acc = acc + wide[i:i + 1, :] * qall[b, h, :, r * lanes:(r + 1) * lanes].astype(F32)
        sums.append(acc)
    acc = jnp.concatenate(sums, axis=0)
    row = jnp.sum(acc.T, axis=0, keepdims=True)
    scores[me] = jnp.broadcast_to(row, scores.shape[1:])

    def score_copy(k, rank):
        return pltpu.make_async_remote_copy(
            src_ref=scores.at[me], dst_ref=scores.at[rank],
            send_sem=s_send.at[k], recv_sem=s_recv.at[rank],
            device_id=peer(k), device_id_type=MESH,
        )

    for k in range(1, ranks):
        score_copy(k, me).start()
    for k in range(1, ranks):
        score_copy(k, lax.rem(me + ranks - k, ranks)).wait_recv()
    total = scores[0, 0:1]
    for r in range(1, ranks):
        total = total + scores[r, 0:1]
    out_ref[...] = total

    for k in range(1, ranks):
        score_copy(k, me).wait_send()
        left_copy(k, me).wait_send()
    for k in range(1, dp):
        q_copy(k, z).wait_send()
        qc_copy(lax.rem(z + dp - k, dp), s).wait_send()


def pieces(total, sizes):
    out, start = [], 0
    for i in range(total):
        if start == total:
            break
        size = min(sizes[min(i, len(sizes) - 1)], total - start)
        out.append((start, size))
        start += size
    return tuple(out)


def solution(mesh):
    shape = dict(mesh.shape)
    groups, dp, tensor, seq = (shape[a] for a in ("groups", "dp", "tensor", "seq"))

    def body(act, gate, grad, down, pin, pout, cin, cout, query):
        tokens, d_local = act.shape[1:]
        features = grad.shape[2]
        ff = down.shape[0]
        pin, pout = pin.T, pout.T
        k1, k2 = pin.shape[0], pout.shape[0]
        nq_block, width = query.shape
        first, second = pieces(ff, (512, 512, 768)), pieces(ff, (1024, 768))
        ranks = tensor * seq
        nq = nq_block * dp
        scale = 1.0 / math.sqrt(gate.shape[1] * k1 * k2)
        dma = pltpu.SemaphoreType.DMA
        scratch = [
            pltpu.VMEM((ff, features), BF16),
            pltpu.VMEM((2, tokens, features), BF16),
            pltpu.VMEM((2, tokens, ff), BF16),
            pltpu.VMEM((tokens, d_local), BF16),
            pltpu.VMEM((k1, d_local), BF16),
            pltpu.VMEM((k2, ff), BF16),
            pltpu.VMEM((k1, k1), F32),
            pltpu.VMEM((k2, k2), F32),
            pltpu.VMEM((nq_block, width), F32),
            pltpu.VMEM((dp, seq, nq_block, width // seq), BF16),
            pltpu.VMEM((ranks, k1, tokens), F32),
            pltpu.VMEM((ranks, 8, nq), F32),
            dma((len(first),)),
            dma((9,)),
            dma((2,)),
            dma((ranks,)), dma((ranks,)),
            dma((dp,)), dma((dp,)),
            dma((dp,)), dma((dp,)),
            dma((ranks,)), dma((ranks,)),
        ]
        return pl.pallas_call(
            functools.partial(kernel, (groups, dp, tensor, seq, first, second), scale),
            out_shape=jax.ShapeDtypeStruct((1, nq), F32),
            in_specs=[pl.BlockSpec(memory_space=pl.ANY)] * 9,
            out_specs=pl.BlockSpec(memory_space=pltpu.VMEM),
            scratch_shapes=scratch,
            compiler_params=pltpu.CompilerParams(
                collective_id=0, has_side_effects=True, vmem_limit_bytes=58 * 2**20
            ),
            cost_estimate=pl.CostEstimate(
                flops=4 * tokens * ff * features,
                bytes_accessed=2 * ff * features,
                transcendentals=0,
            ),
        )(act, gate, grad, down, pin, pout, cin, cout, query)

    return jax.shard_map(
        body,
        mesh=mesh,
        in_specs=(
            P(("groups", "dp"), "seq", "tensor"),
            P(("groups", "dp"), None, ("tensor", "seq")),
            P(("groups", "dp"), "seq", None),
            P(("tensor", "seq"), None),
            P("tensor", None),
            P(("tensor", "seq"), None),
            P(),
            P(),
            P(("groups", "dp"), None),
        ),
        out_specs=P(("groups", "dp"), None),
        check_vma=False,
    )
```
